512 devices in a mesh: dp: 32 (over y, x), tensor: 16 (over z, core).
Axes of the slice: x: 4, y: 8, z: 8, core: 2. Of those that a mesh axis runs over, the one named last changes fastest.
Arguments:
- activations: bfloat16 [90112, 4096], P('dp', 'tensor'), may hold values from -6 to 6
- cotangent: bfloat16 [90112, 4096], P('dp', 'tensor'), may hold values from -6 to 6
- down_adapters: bfloat16 [192, 4096, 64], P('dp', 'tensor'), may hold values from -0.09375 to 0.09375
- up_adapters: bfloat16 [192, 64, 4096], P('dp', None, 'tensor'), may hold values from -0.75 to 0.75
- block_persona: int32 [704], P('dp'), may hold values from 0 to 191, as said below
- persona_slot: int32 [192], replicated, may hold values from 0 to 191, as said below
Outputs:
- grad_input: bfloat16 [90112, 4096], P('dp', 'tensor')
- grad_down: bfloat16 [192, 4096, 64], P('dp', 'tensor')
- grad_up: bfloat16 [192, 64, 4096], P('dp', None, 'tensor')
The draws below stay inside these ranges and needn't reach their ends.
Inputs may be any that keep to these rules, and one draw needn't show every extreme that they name: `block_persona`: among the 22 blocks of one index of dp, at most 2 name personas of one owner; in every draw one owner gets exactly 2 blocks from every index of dp. `persona_slot`: A permutation of the slots.
All inputs are finite; a program needn't handle non-finite values.
Results may differ from the reference program's by a relative error of at most 0.005.
Values may be sent and summed in bfloat16 or wider, within the bound.
A program may use at most 64 MiB of HBM per device.

```python
import jax
import jax.numpy as jnp
from jax import lax

D = 4096
R = 64
PERSONA_BLOCK = 128
PERS_DEV = 6
BLK_DEV = 22
OWNERS = 32
CAP = 2
PERSONAS = 192
BLOCKS = 704
TOKENS = 90112


def routing(key):
    key = jax.random.fold_in(key, 7)
    key_perm, key_heavy, key_prio, key_mixing, key_local = jax.random.split(key, 5)
    slot_of = jax.random.permutation(key_perm, PERSONAS).astype(jnp.int32)
    persona_at = jnp.argsort(slot_of).astype(jnp.int32)
    heavy_owner = jax.random.randint(key_heavy, (), 0, OWNERS)
    item_ids = jnp.arange(OWNERS * CAP, dtype=jnp.int32)
    item_owner = item_ids // CAP

    def shuffle_items(single):
        return jax.random.permutation(single, OWNERS * CAP).astype(jnp.int32)

    def shuffle_blocks(single):
        return jax.random.permutation(single, BLK_DEV).astype(jnp.int32)
    priority = jax.vmap(shuffle_items)(jax.random.split(key_prio, OWNERS))
    scores = jnp.where(item_owner[None, :] == heavy_owner, item_ids[None, :] % CAP - CAP, priority)
    picked = jnp.argsort(scores, axis=1)[:, :BLK_DEV]
    owners_of = item_owner[picked]
    mixing = jax.vmap(shuffle_blocks)(jax.random.split(key_mixing, OWNERS))
    owners_of = jnp.take_along_axis(owners_of, mixing, axis=1)
    local_pick = jax.random.randint(key_local, (OWNERS, BLK_DEV), 0, PERS_DEV)
    block_persona = persona_at[owners_of * PERS_DEV + local_pick].reshape(BLOCKS)
    return (slot_of, block_persona.astype(jnp.int32))


def draw_block_persona(key, part):
    return routing(key)[1]


def draw_persona_slot(key, part):
    return routing(key)[0]


def block_levels(rng, extent, pieces, least, high):
    def one(position, parts):
        draws = jax.random.uniform(jax.random.fold_in(jax.random.fold_in(rng, 6), position), (parts,), jnp.float32, least / len(pieces), high / len(pieces))
        return jnp.repeat(jnp.exp(draws), extent[position] // parts).reshape((-1,) + (1,) * (len(extent) - position - 1))

    level = one(*pieces[0])
    for cut in pieces[1:]:
        level = level * one(*cut)
    return level


def noise(rng, extent, width, limit, shards=(), kind=jnp.bfloat16):
    level = block_levels(rng, extent, shards, -0.22, 0.18) if shards else 1.0
    drawn = jax.random.normal(rng, extent, jnp.float32) * width * level
    return jnp.minimum(jnp.maximum(drawn, -limit), limit).astype(kind)


def setup_inputs(seed: int = 0) -> dict:
    arg_keys = jax.random.split(jax.random.key(seed), 7)
    return {
        "activations": noise(arg_keys[0], (TOKENS, D), 1.0, 6.0, ((0, 32), (1, 16))),
        "cotangent": noise(arg_keys[1], (TOKENS, D), 1.0, 6.0, ((0, 32), (1, 16))),
        "down_adapters": noise(arg_keys[2], (PERSONAS, D, R), D ** -0.5, 0.09375, ((0, 32), (1, 16))),
        "up_adapters": noise(arg_keys[3], (PERSONAS, R, D), R ** -0.5, 0.75, ((0, 32), (2, 16))),
        "block_persona": draw_block_persona(jax.random.fold_in(arg_keys[6], 71), 0),
        "persona_slot": draw_persona_slot(jax.random.fold_in(arg_keys[6], 71), 0),
    }


adapter_scale = 2.0


def reference(activations, cotangent, down_adapters, up_adapters, block_persona, persona_slot):
    slots = persona_slot[block_persona].astype(jnp.int32)
    act_blocks = activations.reshape(BLOCKS, PERSONA_BLOCK, D)
    cot_blocks = cotangent.reshape(BLOCKS, PERSONA_BLOCK, D)

    def advance(carry, item):
        sum_down, sum_up, member_counts = carry
        act_rows, cot_rows, slot_index = item
        down_weight = lax.dynamic_index_in_dim(down_adapters, slot_index, 0, keepdims=False)
        up_mat = lax.dynamic_index_in_dim(up_adapters, slot_index, 0, keepdims=False)
        rank_up = jnp.dot(act_rows, down_weight, preferred_element_type=jnp.float32).astype(jnp.bfloat16)
        rank_gradient = jnp.dot(cot_rows, up_mat.T, preferred_element_type=jnp.float32).astype(jnp.bfloat16)
        gradient_rows = (adapter_scale * jnp.dot(rank_gradient, down_weight.T, preferred_element_type=jnp.float32)).astype(jnp.bfloat16)
        term_down = jnp.dot(act_rows.T, rank_gradient, preferred_element_type=jnp.float32)
        term_up = jnp.dot(rank_up.T, cot_rows, preferred_element_type=jnp.float32)
        sum_down = sum_down.at[slot_index].add(term_down)
        sum_up = sum_up.at[slot_index].add(term_up)
        member_counts = member_counts.at[slot_index].add(jnp.float32(1.0))
        return (sum_down, sum_up, member_counts), gradient_rows

    start = (jnp.zeros((PERSONAS, D, R), jnp.float32), jnp.zeros((PERSONAS, R, D), jnp.float32), jnp.zeros((PERSONAS,), jnp.float32))
    (sum_down, sum_up, member_counts), grad_blocks = lax.scan(advance, start, (act_blocks, cot_blocks, slots))
    scaling_multiplier = adapter_scale / (PERSONA_BLOCK * jnp.maximum(member_counts, 1.0))
    grad_input = grad_blocks.reshape(TOKENS, D)
    grad_down = (sum_down * scaling_multiplier[:, None, None]).astype(jnp.bfloat16)
    grad_up = (sum_up * scaling_multiplier[:, None, None]).astype(jnp.bfloat16)
    return grad_input, grad_down, grad_up
```

```python
import functools

import jax
import jax.numpy as jnp
from jax import lax
from jax.experimental import pallas as pl
from jax.experimental.pallas import tpu as pltpu
from jax.sharding import PartitionSpec as P

MESH = pl.DeviceIdType.MESH
NX = 4
CORES = 2
CAP = 2
ADAPTER_SCALE = 2.0
F32 = jnp.float32
BF16 = jnp.bfloat16


def prep_kernel(ny, pers, blocks, bp, ps, req, blk_slot, slot_blk, used):
    me = lax.axis_index("dp")
    my_y, my_x = me // NX, me % NX
    owners = ny * NX

    def clear(i, _):
        req[0, i] = -1
        slot_blk[0, i] = blocks
        used[i] = 0
        return 0

    lax.fori_loop(0, 128, clear, 0)

    def place(b, _):
        slot = ps[bp[b]]
        owner = slot // pers
        pos = used[owner]
        used[owner] = pos + 1
        s = owner * CAP + pos
        req[0, s] = slot - owner * pers
        slot_blk[0, s] = b
        row = lax.rem(owner // NX - my_y + ny, ny)
        rel = lax.rem(lax.rem(owner, NX) - my_x + NX, NX)
        own = 8 * ny + row * 2 + pos
        right = 3 * ny + row * 3 + pos
        left = row * 3 + pos
        across = 6 * ny + pos * ny + row
        blk_slot[0, b] = jnp.where(
            rel == 0, own, jnp.where(rel == 1, right, jnp.where(rel == 2, across, left))
        )
        return 0

    lax.fori_loop(0, blocks, place, 0)


class Copies:
    def __init__(self, send, recv):
        self.send, self.recv, self.used, self.all = send, recv, 0, []

    def make(self, src, dst, device):
        i = self.used
        self.used += 1
        copy = pltpu.make_async_remote_copy(
            src_ref=src, dst_ref=dst, send_sem=self.send.at[i], recv_sem=self.recv.at[i],
            device_id=device, device_id_type=MESH,
        )
        self.all.append(copy)
        return copy


def copy_count(ny, nz):
    return 2 * ny * 4 * 2 + 2 * (ny - 1) * 2 + 2 * (2 + 2 * (nz - 1)) + (NX - 1) + (ny - 1)


def main_kernel(cfg, *refs):
    ny, nz, pers, blocks, pad_blocks, rank = cfg
    (req_s, blk_slot, slot_blk, req_v, up, down, act, cot, gi, gdn, gup) = refs[:11]
    refs = list(refs[11:])

    def take(n):
        out = refs[:n]
        del refs[:n]
        return out

    act_v, cot_v, gi_v = take(3)
    tab = [[up] + take(ny - 1), take(ny)]
    rx = take(2)
    sx = [take(2), take(2)]
    grads = take(2)
    gr = take(2)
    bs = [take(2), take(2)]
    ys = [take(ny - 1), take(ny - 1)]
    yr = [take(ny - 1), take(ny - 1)]
    part, pair, zs, zr, full = take(2), take(2), take(2), take(2), take(2)
    rtab_v, rtab_s, ctab = take(3)
    send_sem, recv_sem, local_sem = take(3)
    copies = Copies(send_sem, recv_sem)

    dp, tensor = lax.axis_index("dp"), lax.axis_index("tensor")
    y, x = dp // NX, lax.rem(dp, NX)
    z, core = tensor // CORES, lax.rem(tensor, CORES)

    def at_x(d):
        return (y * NX + lax.rem(x + d + NX, NX), tensor)

    def at_y(d):
        return (lax.rem(y + d + ny, ny) * NX + x, tensor)

    def at_z(d):
        return (dp, lax.rem(z + d + nz, nz) * CORES + core)

    sibling = (dp, z * CORES + (1 - core))

    load_act = pltpu.make_async_copy(act, act_v, local_sem.at[0])
    load_cot = pltpu.make_async_copy(cot, cot_v, local_sem.at[1])
    load_act.start()
    load_cot.start()

    barrier = pltpu.get_barrier_semaphore()
    peers = [at_x(d) for d in range(1, NX)] + [at_y(d) for d in range(1, ny)]
    peers += [at_z(d) for d in range(1, nz)] + [sibling]
    for peer in peers:
        pl.semaphore_signal(barrier, inc=1, device_id=peer, device_id_type=MESH)
    pl.semaphore_wait(barrier, len(peers))

    steps_p = [ny // 2, ny - 1 - ny // 2]
    steps_m = [ny - 1 - ny // 2, ny // 2]
    ring = {}

    def ring_send(h, toward_low, step):
        if toward_low:
            src, row, device = tab[h][step - 1], step, at_y(-1)
        else:
            src, row, device = tab[h][(ny - step + 1) % ny], ny - step, at_y(1)
        copy = copies.make(src, tab[h][row], device)
        copy.start()
        ring[h, row] = (copy, toward_low, step)

    def ring_first(h, toward_low):
        if (steps_p if toward_low else steps_m)[h] >= 1:
            ring_send(h, toward_low, 1)

    def ring_take(h, row):
        if row == 0:
            return
        copy, toward_low, step = ring[h, row]
        copy.wait_recv()
        if step < (steps_p if toward_low else steps_m)[h]:
            ring_send(h, toward_low, step + 1)
        elif h == 0:
            ring_first(1, toward_low)

    def ring_order(h):
        order = [0]
        for s in range(1, ny // 2 + 1):
            first = [(s, steps_p[h]), (ny - s, steps_m[h])]
            order += [row for row, steps in first if s <= steps]
        return order

    ask = []
    for d in range(1, NX):
        copy = copies.make(req_v, rtab_v.at[NX - d], at_x(d))
        copy.start()
        ask.append(copy)
    ring_first(0, True)
    ring_first(0, False)
    if steps_m[0] == 0:
        ring_first(1, False)
    rtab_v[0] = req_v[...]

    for k in range(pers):
        tab[1][0][k] = jnp.transpose(down[k])

    for copy in ask:
        copy.wait_recv()
    to_smem = pltpu.make_async_copy(rtab_v, rtab_s, local_sem.at[2])
    to_smem.start()
    ctab[0] = rtab_v[...]
    to_smem.wait()
    table_copies = []
    for d in range(1, ny):
        copy = copies.make(rtab_v, ctab.at[ny - d], at_y(d))
        copy.start()
        table_copies.append(copy)

    def owner_slot(row, rel_x):
        return (lax.rem(y + row, ny) * NX + lax.rem(x + rel_x, NX)) * CAP

    hops = {}

    def x_send(key, land, stage, row):
        for side, d in ((0, 1), (1, -1)):
            copy = copies.make(
                stage[side].at[row], land.at[pl.ds(side * 3 * ny + row * 3, 3)], at_x(d)
            )
            copy.start()
            hops[key, side] = copy

    def x_hand_on(key, land, row):
        for side, d in ((0, 1), (1, -1)):
            hops[key, side].wait_recv()
            copy = copies.make(
                land.at[pl.ds(side * 3 * ny + row * 3 + 2, 1)],
                land.at[pl.ds((6 + side) * ny + row, 1)],
                at_x(d),
            )
            copy.start()
            hops[key, side + 2] = copy

    def x_landed(key):
        hops[key, 2].wait_recv()
        hops[key, 3].wait_recv()

    def issue_adapters(h, row):
        table = tab[h][row]

        def pick(rel_x, pos):
            return table[jnp.maximum(rtab_s[rel_x, 0, owner_slot(row, 0) + pos], 0)]

        for side, rel_x in ((0, 1), (1, NX - 1)):
            stage = sx[h][side]
            stage[row, 0] = pick(rel_x, 0)
            stage[row, 1] = pick(rel_x, 1)
            stage[row, 2] = pick(2, side)
        x_send(("a", h, row), rx[h], sx[h], row)
        for pos in range(CAP):
            rx[h][8 * ny + row * 2 + pos] = pick(0, pos)

    def issue_gradients(h, row):
        def pick(rel_x, pos):
            return grads[h][slot_blk[0, owner_slot(row, rel_x) + pos]]

        for side, rel_x in ((0, 1), (1, NX - 1)):
            stage = bs[h][side]
            stage[row, 0] = pick(rel_x, 0)
            stage[row, 1] = pick(rel_x, 1)
            stage[row, 2] = pick(2, side)
        x_send(("g", h, row), gr[h], bs[h], row)

    sums = {}

    def row_sum(h, row, k):
        base = owner_slot(row, 0)
        total = jnp.zeros((rank, up.shape[2]), F32)
        places = [(3, row * 3), (1, 3 * ny + row * 3)]
        terms = []
        for rel_x, first in places:
            for pos in range(CAP):
                terms.append((rtab_s[rel_x, 0, base + pos], gr[h][first + pos]))
        terms.append((rtab_s[2, 0, base], gr[h][6 * ny + row]))
        terms.append((rtab_s[2, 0, base + 1], gr[h][7 * ny + row]))
        for pos in range(CAP):
            terms.append((rtab_s[0, 0, base + pos], grads[h][slot_blk[0, base + pos]]))
        for asked, term in terms:
            total += jnp.where(asked == k, term.astype(F32), 0.0)
        return total

    back_p = [steps_p[1], steps_p[0]]
    back_m = [steps_m[1], steps_m[0]]

    def back_place(h, row):
        j = ny - row
        return (True, j) if j <= back_p[h] else (False, row)

    def back_slot(toward_low, j):
        return j - 1 if toward_low else ny - 1 - j

    def back_order(h):
        order = []
        for j in range(ny // 2, 0, -1):
            order += [ny - j] if j <= back_p[h] else []
            order += [j] if j <= back_m[h] else []
        return order + [0]

    def finish_gradients(h, row):
        x_landed(("g", h, row))
        if row == 0:
            return
        toward_low, j = back_place(h, row)
        farther = None
        if j < (back_p if toward_low else back_m)[h]:
            sums[h, toward_low, j + 1].wait_recv()
            farther = yr[h][back_slot(toward_low, j + 1)]
        out = ys[h][back_slot(toward_low, j)]

        def one(k, _):
            total = row_sum(h, row, k)
            if farther is not None:
                total += farther[k].astype(F32)
            out[k] = total.astype(BF16)
            return 0

        lax.fori_loop(0, pers, one, 0)
        copy = copies.make(out, yr[h][back_slot(toward_low, j)], at_y(-1 if toward_low else 1))
        copy.start()
        sums[h, toward_low, j] = copy

    def write_gradients(h):
        nearest = []
        for toward_low in (True, False):
            if (back_p if toward_low else back_m)[h] >= 1:
                sums[h, toward_low, 1].wait_recv()
                nearest.append(yr[h][back_slot(toward_low, 1)])
        lane = lax.broadcasted_iota(jnp.int32, (1, 128), 1)
        mine = lane // CAP == dp
        for k in range(pers):
            hits = jnp.zeros((1, 128), F32)
            for other in range(ny):
                for rel_x in range(NX):
                    hits += jnp.where(mine & (ctab[other, rel_x] == k), 1.0, 0.0)
            count = jnp.sum(hits, axis=1, keepdims=True)
            scaling = ADAPTER_SCALE / (act.shape[1] * jnp.maximum(count, 1.0))
            total = row_sum(h, 0, k)
            for ref in nearest:
                total += ref[k].astype(F32)
            total = total * scaling
            if h == 0:
                gdn[k] = jnp.transpose(total).astype(BF16)
            else:
                gup[k] = total.astype(BF16)

    half = pad_blocks * rank // 2
    chunk = half // nz
    tensor_copies = {}

    def rows_of(c, zz):
        return pl.ds(pl.multiple_of(c * half + zz * chunk, 16), chunk)

    def project(h):
        if h == 0:
            load_cot.wait()
        for row in range(ny):
            x_landed(("a", h, row))
        tokens = cot_v if h == 0 else act_v

        def one(b, _):
            weights = rx[h][blk_slot[0, b]]
            part[h][pl.ds(pl.multiple_of(b * rank, rank), rank), :] = lax.dot_general(
                weights, tokens[b], (((1,), (1,)), ((), ())), preferred_element_type=F32
            )
            return 0

        lax.fori_loop(0, blocks, one, 0, unroll=2)
        if pad_blocks > blocks:
            part[h][pl.ds(blocks * rank, (pad_blocks - blocks) * rank), :] = jnp.zeros(
                ((pad_blocks - blocks) * rank, part[h].shape[1]), F32
            )
        copy = copies.make(
            part[h].at[pl.ds(pl.multiple_of((1 - core) * half, 16), half)], pair[h], sibling
        )
        copy.start()
        tensor_copies[h, "pair"] = copy

    def scatter(h):
        tensor_copies[h, "pair"].wait_recv()

        def one(zz, _):
            rows = pl.ds(pl.multiple_of(zz * chunk, 16), chunk)
            zs[h][rows, :] = (part[h][rows_of(core, zz), :] + pair[h][rows, :]).astype(BF16)
            return 0

        lax.fori_loop(0, nz, one, 0)
        for d in range(1, nz):
            other = lax.rem(z + d, nz)
            copy = copies.make(
                zs[h].at[pl.ds(pl.multiple_of(other * chunk, 16), chunk)], zr[h].at[d - 1], at_z(d)
            )
            copy.start()
            tensor_copies[h, "scatter", d] = copy

    def gather(h):
        own = pl.ds(pl.multiple_of(z * chunk, 16), chunk)
        total = part[h][rows_of(core, z), :] + pair[h][own, :]
        for d in range(1, nz):
            tensor_copies[h, "scatter", d].wait_recv()
            total += zr[h][d - 1].astype(F32)
        mine = rows_of(core, z)
        full[h][mine, :] = total.astype(BF16)
        for d in range(1, nz):
            copy = copies.make(full[h].at[mine], full[h].at[mine], at_z(d))
            copy.start()
            tensor_copies[h, "gather", d] = copy

    def share(h):
        for d in range(1, nz):
            tensor_copies[h, "gather", d].wait_recv()
        mine = pl.ds(pl.multiple_of(core * half, 16), half)
        copy = copies.make(full[h].at[mine], full[h].at[mine], sibling)
        copy.start()
        tensor_copies[h, "share"] = copy

    def ranks(h, b):
        return full[h][pl.ds(pl.multiple_of(b * rank, rank), rank), :]

    def block_gradients(h):
        tensor_copies[h, "share"].wait_recv()
        if h == 0:
            load_act.wait()
        tokens = act_v if h == 0 else cot_v
        grads[h][blocks] = jnp.zeros(grads[h].shape[1:], BF16)

        def one(b, _):
            grads[h][b] = jnp.dot(ranks(h, b), tokens[b], preferred_element_type=F32).astype(BF16)
            return 0

        lax.fori_loop(0, blocks, one, 0, unroll=2)

    store_gi = pltpu.make_async_copy(gi_v, gi, local_sem.at[3])

    def input_gradient():
        def one(b, _):
            weights = rx[1][blk_slot[0, b]]
            gi_v[b] = (
                ADAPTER_SCALE
                * lax.dot_general(
                    ranks(0, b), weights, (((0,), (0,)), ((), ())), preferred_element_type=F32
                )
            ).astype(BF16)
            return 0

        lax.fori_loop(0, blocks, one, 0, unroll=2)
        store_gi.start()

    jobs = [("a", h, row) for h in (0, 1) for row in ring_order(h)]
    jobs += [("g", h, row) for h in (0, 1) for row in back_order(h)]
    lead, lag, finish_lag = 2, 1, 2
    hooks = {}

    def hook(i, *what):
        hooks.setdefault(i, []).extend(what)

    for h, start in ((0, ny), (1, 2 * ny)):
        stages = [project, scatter, gather, share]
        for j, stage in enumerate(stages):
            hook(start + 2 + (ny - 2) * j // len(stages), functools.partial(stage, h))
            if h == 1 and j == 1:
                hook(start + 2 + (ny - 2) * j // len(stages), input_gradient)
        hook(start + ny, functools.partial(block_gradients, h))
    hook(3 * ny + finish_lag, lambda: write_gradients(0))

    taken = 0
    for i in range(len(jobs) + finish_lag):
        while taken < min(i + lead + 1, 2 * ny):
            ring_take(*jobs[taken][1:])
            taken += 1
        for what in hooks.get(i, []):
            what()
        if i < len(jobs):
            kind, h, row = jobs[i]
            (issue_adapters if kind == "a" else issue_gradients)(h, row)
        if 0 <= i - lag < len(jobs):
            kind, h, row = jobs[i - lag]
            x_hand_on((kind, h, row), rx[h] if kind == "a" else gr[h], row)
        if 0 <= i - finish_lag < len(jobs):
            kind, h, row = jobs[i - finish_lag]
            if kind == "g":
                finish_gradients(h, row)
        if i == 0:
            for copy in table_copies:
                copy.wait_recv()
    write_gradients(1)
    for copy in copies.all:
        copy.wait_send()
    store_gi.wait()
    assert copies.used == copy_count(ny, nz)


def step(ny, nz, activations, cotangent, down_adapters, up_adapters, block_persona, persona_slot):
    blocks = block_persona.shape[0]
    block = activations.shape[0] // blocks
    features = activations.shape[1]
    pers, rank = up_adapters.shape[:2]
    smem = pl.BlockSpec(memory_space=pltpu.SMEM)
    vmem = pl.BlockSpec(memory_space=pltpu.VMEM)
    anywhere = pl.BlockSpec(memory_space=pl.ANY)
    line = jax.ShapeDtypeStruct((1, 128), jnp.int32)
    req, blk_slot, slot_blk = pl.pallas_call(
        functools.partial(prep_kernel, ny, pers, blocks),
        out_shape=(line, line, line),
        in_specs=[smem, smem],
        out_specs=(smem, smem, smem),
        scratch_shapes=[pltpu.SMEM((128,), jnp.int32)],
    )(block_persona, persona_slot)

    unit = CORES * nz * 16
    pad_blocks = blocks
    while pad_blocks * rank % unit:
        pad_blocks += 1
    rows = pad_blocks * rank
    adapter = (rank, features)

    def bf16(*shape):
        return pltpu.VMEM(shape, BF16)

    def f32(*shape):
        return pltpu.VMEM(shape, F32)

    scratch = [bf16(blocks, block, features)] * 3
    scratch += [bf16(pers, *adapter)] * (2 * ny - 1)
    scratch += [bf16(10 * ny, *adapter)] * 2
    scratch += [bf16(ny, 3, *adapter)] * 4
    scratch += [bf16(blocks + 1, *adapter)] * 2
    scratch += [bf16(8 * ny, *adapter)] * 2
    scratch += [bf16(ny, 3, *adapter)] * 4
    scratch += [bf16(pers, *adapter)] * (4 * (ny - 1))
    scratch += [f32(rows, block)] * 2 + [f32(rows // 2, block)] * 2
    scratch += [bf16(rows // 2, block)] * 2
    scratch += [bf16(max(nz - 1, 1), rows // 2 // nz, block)] * 2
    scratch += [bf16(rows, block)] * 2
    scratch += [
        pltpu.VMEM((NX, 1, 128), jnp.int32),
        pltpu.SMEM((NX, 1, 128), jnp.int32),
        pltpu.VMEM((ny, NX, 1, 128), jnp.int32),
    ]
    n = copy_count(ny, nz)
    scratch += [pltpu.SemaphoreType.DMA((n,)), pltpu.SemaphoreType.DMA((n,)), pltpu.SemaphoreType.DMA((4,))]
    gi, gdn, gup = pl.pallas_call(
        functools.partial(main_kernel, (ny, nz, pers, blocks, pad_blocks, rank)),
        out_shape=(
            jax.ShapeDtypeStruct((blocks, block, features), BF16),
            jax.ShapeDtypeStruct(down_adapters.shape, BF16),
            jax.ShapeDtypeStruct(up_adapters.shape, BF16),
        ),
        in_specs=[smem, smem, smem, vmem, vmem, vmem, anywhere, anywhere],
        out_specs=(anywhere, vmem, vmem),
        scratch_shapes=scratch,
        compiler_params=pltpu.CompilerParams(
            collective_id=0, has_side_effects=True, vmem_limit_bytes=56 * 2**20
        ),
    )(
        req, blk_slot, slot_blk, req, up_adapters, down_adapters,
        activations.reshape(blocks, block, features), cotangent.reshape(blocks, block, features),
    )
    return gi.reshape(activations.shape), gdn, gup


def solution(mesh):
    ny, nz = mesh.shape["dp"] // NX, mesh.shape["tensor"] // CORES
    return jax.shard_map(
        functools.partial(step, ny, nz),
        mesh=mesh,
        in_specs=(
            P("dp", "tensor"),
            P("dp", "tensor"),
            P("dp", "tensor", None),
            P("dp", None, "tensor"),
            P("dp"),
            P(),
        ),
        out_specs=(P("dp", "tensor"), P("dp", "tensor", None), P("dp", None, "tensor")),
        check_vma=False,
    )
```

```python
import functools

import jax
import jax.numpy as jnp
from jax import lax
from jax.experimental import pallas as pl
from jax.experimental.pallas import tpu as pltpu
from jax.sharding import PartitionSpec as P

MESH = pl.DeviceIdType.MESH
NX = 4
CORES = 2
CAP = 2
CHUNKS = 2
ADAPTER_SCALE = 2.0
F32 = jnp.float32
BF16 = jnp.bfloat16


class Copies:
    def __init__(self, send, recv):
        self.send, self.recv, self.used, self.all = send, recv, 0, []

    def make(self, src, dst, device):
        i = self.used
        self.used += 1
        copy = pltpu.make_async_remote_copy(
            src_ref=src, dst_ref=dst, send_sem=self.send.at[i], recv_sem=self.recv.at[i],
            device_id=device, device_id_type=MESH,
        )
        self.all.append(copy)
        return copy

    def flush(self, count):
        for copy in self.all[:count]:
            copy.wait_send()
        self.all = self.all[count:]


def copy_count(ny, nz):
    return 4 * ny * (NX - 1) + 4 * (ny - 1) * CHUNKS + 2 * (2 + 2 * (nz - 1)) + (NX - 1) + (ny - 1)


def main_kernel(cfg, *refs):
    ny, nz, pers, blocks, pad_blocks, rank = cfg
    (bp, ps, up_in, down_in, act, cot, gi, gdn, gup) = refs[:9]
    refs = list(refs[9:])

    def take(n):
        out = refs[:n]
        del refs[:n]
        return out

    act_v, cot_v, gi_v = take(3)
    tab = [take(ny), take(ny)]
    rx = take(2)
    sx = [take(NX - 1), take(NX - 1)]
    grads = take(2)
    gr = take(2)
    bs = [take(NX - 1), take(NX - 1)]
    ys = [take(ny - 1), take(ny - 1)]
    yr = [take(ny - 1), take(ny - 1)]
    part, pair, zs, zr, full = take(2), take(2), take(2), take(2), take(2)
    rtab_v, rtab_s, ctab, asked_v, asked_s, blk_slot = take(6)
    send_sem, recv_sem, local_sem = take(3)
    copies = Copies(send_sem, recv_sem)

    dp, tensor = lax.axis_index("dp"), lax.axis_index("tensor")
    y, x = dp // NX, lax.rem(dp, NX)
    z, core = tensor // CORES, lax.rem(tensor, CORES)

    def at_x(d):
        return (y * NX + lax.rem(x + d + NX, NX), tensor)

    def at_y(d):
        return (lax.rem(y + d + ny, ny) * NX + x, tensor)

    def at_z(d):
        return (dp, lax.rem(z + d + nz, nz) * CORES + core)

    sibling = (dp, z * CORES + (1 - core))

    load_act = pltpu.make_async_copy(act, act_v, local_sem.at[0])
    load_cot = pltpu.make_async_copy(cot, cot_v, local_sem.at[1])
    load_up = pltpu.make_async_copy(up_in, tab[0][0], local_sem.at[4])
    load_down = pltpu.make_async_copy(down_in, tab[1][0], local_sem.at[5])
    load_up.start()
    load_down.start()
    load_cot.start()
    load_act.start()

    barrier = pltpu.get_barrier_semaphore()
    peers = [at_x(d) for d in range(1, NX)] + [at_y(d) for d in range(1, ny)]
    peers += [at_z(d) for d in range(1, nz)] + [sibling]
    for peer in peers:
        pl.semaphore_signal(barrier, inc=1, device_id=peer, device_id_type=MESH)

    lane = lax.broadcasted_iota(jnp.int32, (1, 128), 1)
    req = jnp.full((1, 128), -1, jnp.int32)
    asked = jnp.full((1, 128), blocks, jnp.int32)
    owners = []
    for b in range(blocks):
        persona = jnp.clip(bp[b], 0, ps.shape[0] - 1)
        slot = jnp.clip(ps[persona], 0, ps.shape[0] - 1)
        owner = lax.div(slot, pers)
        pos = sum([(owner == other).astype(jnp.int32) for other in owners], jnp.int32(0))
        pos = jnp.minimum(pos, CAP - 1)
        owners.append(owner)
        here = lane == owner * CAP + pos
        req = jnp.where(here, slot - owner * pers, req)
        asked = jnp.where(here, b, asked)
        owner_y = lax.div(owner, NX)
        rel_y = lax.rem(owner_y - y + ny, ny)
        rel_x = lax.rem(owner - owner_y * NX - x + NX, NX)
        blk_slot[b] = (rel_x * ny + rel_y) * CAP + pos
    rtab_v[0] = req
    asked_v[...] = asked
    ask_to_smem = pltpu.make_async_copy(asked_v, asked_s, local_sem.at[6])
    ask_to_smem.start()

    pl.semaphore_wait(barrier, len(peers))

    steps_p = [ny // 2, ny - 1 - ny // 2]
    steps_m = [ny - 1 - ny // 2, ny // 2]
    ring = {}
    cut = pers // CHUNKS
    parts = [pl.ds(c * cut, cut if c < CHUNKS - 1 else pers - c * cut) for c in range(CHUNKS)]

    def ring_send(h, toward_low, step, c):
        if toward_low:
            src, row, device = tab[h][step - 1], step, at_y(-1)
        else:
            src, row, device = tab[h][(ny - step + 1) % ny], ny - step, at_y(1)
        copy = copies.make(src.at[parts[c]], tab[h][row].at[parts[c]], device)
        copy.start()
        ring[h, toward_low, step, c] = copy

    def ring_steps(h, toward_low):
        return (steps_p if toward_low else steps_m)[h]

    def ring_first(h, toward_low, c):
        if ring_steps(h, toward_low) >= 1:
            ring_send(h, toward_low, 1, c)

    def ring_take(h, step):
        for c in range(CHUNKS):
            for toward_low in (True, False):
                if step > ring_steps(h, toward_low):
                    continue
                ring[h, toward_low, step, c].wait_recv()
                if step < ring_steps(h, toward_low):
                    ring_send(h, toward_low, step + 1, c)
                if h == 0 and step == max(ring_steps(0, toward_low) - 1, 1):
                    ring_first(1, toward_low, c)
        low = [step] if step <= ring_steps(h, True) else []
        return low + ([ny - step] if step <= ring_steps(h, False) else [])

    ask = []
    for d in range(1, NX):
        copy = copies.make(rtab_v.at[0], rtab_v.at[NX - d], at_x(d))
        copy.start()
        ask.append(copy)
    load_up.wait()
    load_down.wait()
    for c in range(CHUNKS):
        ring_first(0, True, c)
        ring_first(0, False, c)
        if steps_m[0] == 0:
            ring_first(1, False, c)
    for copy in ask:
        copy.wait_recv()
    to_smem = pltpu.make_async_copy(rtab_v, rtab_s, local_sem.at[2])
    to_smem.start()
    ctab[0] = rtab_v[...]
    to_smem.wait()
    ask_to_smem.wait()
    table_copies = []
    for d in range(1, ny):
        copy = copies.make(rtab_v, ctab.at[ny - d], at_y(d))
        copy.start()
        table_copies.append(copy)

    def owner_slot(row, rel_x):
        return (lax.rem(y + row, ny) * NX + lax.rem(x + rel_x, NX)) * CAP

    hops = {}

    def land_at(rel_x, row):
        return pl.ds((rel_x * ny + row) * CAP, CAP)

    def x_send(key, land, stage, row):
        for d in (2, 1, 3):
            copy = copies.make(stage[d - 1].at[row], land.at[land_at(NX - d, row)], at_x(d))
            copy.start()
            hops[key, d] = copy

    def x_landed(key):
        for d in range(1, NX):
            hops[key, d].wait_recv()

    def issue_adapters(h, row):
        table = tab[h][row]

        def pick(rel_x, pos):
            return table[jnp.maximum(rtab_s[rel_x, 0, owner_slot(row, 0) + pos], 0)]

        for d in range(1, NX):
            for pos in range(CAP):
                sx[h][d - 1][row, pos] = pick(d, pos)
        x_send(("a", h, row), rx[h], sx[h], row)
        for pos in range(CAP):
            rx[h][row * CAP + pos] = pick(0, pos)

    def issue_gradients(h, row):
        for d in range(1, NX):
            for pos in range(CAP):
                bs[h][d - 1][row, pos] = grads[h][asked_s[0, owner_slot(row, d) + pos]]
        x_send(("g", h, row), gr[h], bs[h], row)

    sums = {}

    def row_sum(h, row, k):
        base = owner_slot(row, 0)
        total = jnp.zeros((rank, gup.shape[2]), F32)
        terms = []
        for rel_x in range(1, NX):
            for pos in range(CAP):
                place = (rel_x * ny + row) * CAP + pos
                terms.append((rtab_s[rel_x, 0, base + pos], gr[h][place]))
        for pos in range(CAP):
            terms.append((rtab_s[0, 0, base + pos], grads[h][asked_s[0, base + pos]]))
        for asked, term in terms:
            total += jnp.where(asked == k, term.astype(F32), 0.0)
        return total

    back_p = [steps_p[1], steps_p[0]]
    back_m = [steps_m[1], steps_m[0]]

    def back_place(h, row):
        j = ny - row
        return (True, j) if j <= back_p[h] else (False, row)

    def back_slot(toward_low, j):
        return j - 1 if toward_low else ny - 1 - j

    def back_order(h):
        order = []
        for j in range(ny // 2, 0, -1):
            order += [ny - j] if j <= back_p[h] else []
            order += [j] if j <= back_m[h] else []
        return order + [0]

    def finish_gradients(h, row):
        x_landed(("g", h, row))
        if row == 0:
            return
        toward_low, j = back_place(h, row)
        last = j == (back_p if toward_low else back_m)[h]
        farther = None if last else yr[h][back_slot(toward_low, j + 1)]
        out = ys[h][back_slot(toward_low, j)]
        land = yr[h][back_slot(toward_low, j)]

        def one(k, _):
            total = row_sum(h, row, k)
            if farther is not None:
                total += farther[k].astype(F32)
            out[k] = total.astype(BF16)
            return 0

        for c, part in enumerate(parts):
            if not last:
                sums[h, toward_low, j + 1, c].wait_recv()
            lax.fori_loop(part.start, part.start + part.size, one, 0)
            copy = copies.make(out.at[part], land.at[part], at_y(-1 if toward_low else 1))
            copy.start()
            sums[h, toward_low, j, c] = copy

    def write_gradients(h):
        nearest = []
        for toward_low in (True, False):
            if (back_p if toward_low else back_m)[h] >= 1:
                for c in range(CHUNKS):
                    sums[h, toward_low, 1, c].wait_recv()
                nearest.append(yr[h][back_slot(toward_low, 1)])
        mine = lane // CAP == dp
        for k in range(pers):
            hits = jnp.zeros((1, 128), F32)
            for other in range(ny):
                for rel_x in range(NX):
                    hits += jnp.where(mine & (ctab[other, rel_x] == k), 1.0, 0.0)
            count = jnp.sum(hits, axis=1, keepdims=True)
            scaling = ADAPTER_SCALE / (act.shape[1] * jnp.maximum(count, 1.0))
            total = row_sum(h, 0, k)
            for ref in nearest:
                total += ref[k].astype(F32)
            total = total * scaling
            if h == 0:
                gdn[k] = total.astype(BF16)
            else:
                gup[k] = total.astype(BF16)

    half = pad_blocks * rank // 2
    chunk = half // nz
    tensor_copies = {}

    def rows_of(c, zz):
        return pl.ds(pl.multiple_of(c * half + zz * chunk, 16), chunk)

    def project(h):
        if h == 0:
            load_cot.wait()
        for row in range(ny):
            x_landed(("a", h, row))
        tokens = cot_v if h == 0 else act_v

        def one(b, _):
            weights = rx[h][blk_slot[b]]
            part[h][pl.ds(pl.multiple_of(b * rank, rank), rank), :] = lax.dot_general(
                weights, tokens[b], (((1,), (1,)), ((), ())), preferred_element_type=F32
            )
            return 0

        lax.fori_loop(0, blocks, one, 0, unroll=2)
        if pad_blocks > blocks:
            part[h][pl.ds(blocks * rank, (pad_blocks - blocks) * rank), :] = jnp.zeros(
                ((pad_blocks - blocks) * rank, part[h].shape[1]), F32
            )
        copy = copies.make(
            part[h].at[pl.ds(pl.multiple_of((1 - core) * half, 16), half)], pair[h], sibling
        )
        copy.start()
        tensor_copies[h, "pair"] = copy

    def scatter(h):
        tensor_copies[h, "pair"].wait_recv()

        def one(zz, _):
            rows = pl.ds(pl.multiple_of(zz * chunk, 16), chunk)
            zs[h][rows, :] = (part[h][rows_of(core, zz), :] + pair[h][rows, :]).astype(BF16)
            return 0

        lax.fori_loop(0, nz, one, 0)
        for d in range(1, nz):
            other = lax.rem(z + d, nz)
            copy = copies.make(
                zs[h].at[pl.ds(pl.multiple_of(other * chunk, 16), chunk)], zr[h].at[d - 1], at_z(d)
            )
            copy.start()
            tensor_copies[h, "scatter", d] = copy

    def gather(h):
        own = pl.ds(pl.multiple_of(z * chunk, 16), chunk)
        total = part[h][rows_of(core, z), :] + pair[h][own, :]
        for d in range(1, nz):
            tensor_copies[h, "scatter", d].wait_recv()
            total += zr[h][d - 1].astype(F32)
        mine = rows_of(core, z)
        full[h][mine, :] = total.astype(BF16)
        for d in range(1, nz):
            copy = copies.make(full[h].at[mine], full[h].at[mine], at_z(d))
            copy.start()
            tensor_copies[h, "gather", d] = copy

    def share(h):
        for d in range(1, nz):
            tensor_copies[h, "gather", d].wait_recv()
        mine = pl.ds(pl.multiple_of(core * half, 16), half)
        copy = copies.make(full[h].at[mine], full[h].at[mine], sibling)
        copy.start()
        tensor_copies[h, "share"] = copy

    def ranks(h, b):
        return full[h][pl.ds(pl.multiple_of(b * rank, rank), rank), :]

    def block_gradients(h):
        tensor_copies[h, "share"].wait_recv()
        if h == 0:
            load_act.wait()
        tokens = act_v if h == 0 else cot_v
        grads[h][blocks] = jnp.zeros(grads[h].shape[1:], BF16)

        def one(b, _):
            grads[h][b] = jnp.dot(ranks(h, b), tokens[b], preferred_element_type=F32).astype(BF16)
            return 0

        lax.fori_loop(0, blocks, one, 0, unroll=2)

    store_gi = pltpu.make_async_copy(gi_v, gi, local_sem.at[3])

    def input_gradient():
        def one(b, _):
            weights = rx[1][blk_slot[b]]
            gi_v[b] = (
                ADAPTER_SCALE
                * lax.dot_general(
                    ranks(0, b), weights, (((0,), (0,)), ((), ())), preferred_element_type=F32
                )
            ).astype(BF16)
            return 0

        lax.fori_loop(0, blocks, one, 0, unroll=2)
        store_gi.start()

    issue_adapters(0, 0)
    for s in range(1, ny // 2 + 1):
        for row in ring_take(0, s):
            issue_adapters(0, row)
    issue_adapters(1, 0)
    for copy in table_copies:
        copy.wait_recv()
    beside = [(2, project), (3, scatter), (4, gather), (4, share), (99, block_gradients)]
    for s in range(1, ny // 2 + 1):
        for row in ring_take(1, s):
            issue_adapters(1, row)
        while s >= beside[0][0]:
            beside.pop(0)[1](0)
    for _, what in beside:
        what(0)
    early = len(copies.all)
    orders = [back_order(0), back_order(1)]
    for row in orders[0][: ny // 2]:
        issue_gradients(0, row)
    project(1)
    for row in orders[0][ny // 2 :]:
        issue_gradients(0, row)
    scatter(1)

    def turn():
        block_gradients(1)
        for row in orders[1]:
            issue_gradients(1, row)
        copies.flush(early)

    beside = [
        (1, lambda: gather(1)), (2, input_gradient), (3, lambda: share(1)), (4, turn),
    ]
    for i, row in enumerate(orders[0]):
        finish_gradients(0, row)
        while beside and i >= beside[0][0]:
            beside.pop(0)[1]()
    for _, what in beside:
        what()
    write_gradients(0)
    middle = len(copies.all)
    for i, row in enumerate(orders[1]):
        if i == ny - 2:
            copies.flush(middle)
        finish_gradients(1, row)
    write_gradients(1)
    copies.flush(len(copies.all))
    store_gi.wait()
    assert copies.used == copy_count(ny, nz)


def step(ny, nz, activations, cotangent, down_adapters, up_adapters, block_persona, persona_slot):
    blocks = block_persona.shape[0]
    block = activations.shape[0] // blocks
    features = activations.shape[1]
    pers, rank = up_adapters.shape[:2]
    smem = pl.BlockSpec(memory_space=pltpu.SMEM)
    vmem = pl.BlockSpec(memory_space=pltpu.VMEM)
    anywhere = pl.BlockSpec(memory_space=pl.ANY)
    unit = CORES * nz * 16
    pad_blocks = blocks
    while pad_blocks * rank % unit:
        pad_blocks += 1
    rows = pad_blocks * rank
    adapter = (rank, features)

    def bf16(*shape):
        return pltpu.VMEM(shape, BF16)

    def f32(*shape):
        return pltpu.VMEM(shape, F32)

    scratch = [bf16(blocks, block, features)] * 3
    landing = NX * ny * CAP
    scratch += [bf16(pers, *adapter)] * (2 * ny)
    scratch += [bf16(landing, *adapter)] * 2
    scratch += [bf16(ny, CAP, *adapter)] * (2 * (NX - 1))
    scratch += [bf16(blocks + 1, *adapter)] * 2
    scratch += [bf16(landing, *adapter)] * 2
    scratch += [bf16(ny, CAP, *adapter)] * (2 * (NX - 1))
    scratch += [bf16(pers, *adapter)] * (4 * (ny - 1))
    scratch += [f32(rows, block)] * 2 + [f32(rows // 2, block)] * 2
    scratch += [bf16(rows // 2, block)] * 2
    scratch += [bf16(max(nz - 1, 1), rows // 2 // nz, block)] * 2
    scratch += [bf16(rows, block)] * 2
    scratch += [
        pltpu.VMEM((NX, 1, 128), jnp.int32),
        pltpu.SMEM((NX, 1, 128), jnp.int32),
        pltpu.VMEM((ny, NX, 1, 128), jnp.int32),
        pltpu.VMEM((1, 128), jnp.int32),
        pltpu.SMEM((1, 128), jnp.int32),
        pltpu.SMEM((blocks,), jnp.int32),
    ]
    n = copy_count(ny, nz)
    scratch += [pltpu.SemaphoreType.DMA((n,)), pltpu.SemaphoreType.DMA((n,)), pltpu.SemaphoreType.DMA((7,))]
    gi, gdn, gup = pl.pallas_call(
        functools.partial(main_kernel, (ny, nz, pers, blocks, pad_blocks, rank)),
        out_shape=(
            jax.ShapeDtypeStruct((blocks, block, features), BF16),
            jax.ShapeDtypeStruct(up_adapters.shape, BF16),
            jax.ShapeDtypeStruct(up_adapters.shape, BF16),
        ),
        in_specs=[smem, smem] + [anywhere] * 4,
        out_specs=(anywhere, vmem, vmem),
        scratch_shapes=scratch,
        compiler_params=pltpu.CompilerParams(
            collective_id=0, has_side_effects=True, vmem_limit_bytes=56 * 2**20
        ),
    )(
        block_persona, persona_slot, up_adapters, jnp.swapaxes(down_adapters, 1, 2),
        activations.reshape(blocks, block, features), cotangent.reshape(blocks, block, features),
    )
    return gi.reshape(activations.shape), jnp.swapaxes(gdn, 1, 2), gup


def solution(mesh):
    ny, nz = mesh.shape["dp"] // NX, mesh.shape["tensor"] // CORES
    return jax.shard_map(
        functools.partial(step, ny, nz),
        mesh=mesh,
        in_specs=(
            P("dp", "tensor"),
            P("dp", "tensor"),
            P("dp", "tensor", None),
            P("dp", None, "tensor"),
            P("dp"),
            P(),
        ),
        out_specs=(P("dp", "tensor"), P("dp", "tensor", None), P("dp", None, "tensor")),
        check_vma=False,
    )
```

```python
import functools

import jax
import jax.numpy as jnp
from jax import lax
from jax.experimental import pallas as pl
from jax.experimental.pallas import tpu as pltpu
from jax.sharding import PartitionSpec as P

MESH = pl.DeviceIdType.MESH
NX = 4
CORES = 2
CAP = 2
CHUNKS = 2
ADAPTER_SCALE = 2.0
F32 = jnp.float32
BF16 = jnp.bfloat16


class Copies:
    def __init__(self, send, recv):
        self.send, self.recv, self.used, self.all = send, recv, 0, []

    def make(self, src, dst, device):
        i = self.used
        self.used += 1
        copy = pltpu.make_async_remote_copy(
            src_ref=src, dst_ref=dst, send_sem=self.send.at[i], recv_sem=self.recv.at[i],
            device_id=device, device_id_type=MESH,
        )
        self.all.append(copy)
        return copy

    def flush(self, count):
        for copy in self.all[:count]:
            copy.wait_send()
        self.all = self.all[count:]


def copy_count(ny, nz):
    return 4 * ny * (NX - 1) + 4 * (ny - 1) * CHUNKS + 2 * (1 + nz + 2 * (nz - 1)) + (NX - 1) + (ny - 1)


def main_kernel(cfg, *refs):
    ny, nz, pers, blocks, pad_blocks, rank = cfg
    (bp, ps, up_in, down_in, act, cot, gi, gdn, gup) = refs[:9]
    refs = list(refs[9:])

    def take(n):
        out = refs[:n]
        del refs[:n]
        return out

    act_v, cot_v, gi_v = take(3)
    tab = [take(ny), take(ny)]
    rx = take(2)
    sx = [take(NX - 1), take(NX - 1)]
    grads = take(2)
    gr = take(2)
    bs = [take(NX - 1), take(NX - 1)]
    ys = [take(ny - 1), take(ny - 1)]
    yr = [take(ny - 1), take(ny - 1)]
    part, pair, zs, zr, full = take(2), take(2), take(2), take(2), take(2)
    rtab_v, rtab_s, ctab, asked_v, asked_s, blk_slot = take(6)
    send_sem, recv_sem, local_sem = take(3)
    copies = Copies(send_sem, recv_sem)

    dp, tensor = lax.axis_index("dp"), lax.axis_index("tensor")
    y, x = dp // NX, lax.rem(dp, NX)
    z, core = tensor // CORES, lax.rem(tensor, CORES)

    def at_x(d):
        return (y * NX + lax.rem(x + d + NX, NX), tensor)

    def at_y(d):
        return (lax.rem(y + d + ny, ny) * NX + x, tensor)

    def at_z(d):
        return (dp, lax.rem(z + d + nz, nz) * CORES + core)

    sibling = (dp, z * CORES + (1 - core))

    load_act = pltpu.make_async_copy(act, act_v, local_sem.at[0])
    load_cot = pltpu.make_async_copy(cot, cot_v, local_sem.at[1])
    load_up = pltpu.make_async_copy(up_in, tab[0][0], local_sem.at[4])
    load_down = pltpu.make_async_copy(down_in, tab[1][0], local_sem.at[5])
    load_up.start()
    load_down.start()
    load_cot.start()
    load_act.start()

    barrier = pltpu.get_barrier_semaphore()
    peers = [at_x(d) for d in range(1, NX)] + [at_y(d) for d in range(1, ny)]
    peers += [at_z(d) for d in range(1, nz)] + [sibling]
    for peer in peers:
        pl.semaphore_signal(barrier, inc=1, device_id=peer, device_id_type=MESH)

    lane = lax.broadcasted_iota(jnp.int32, (1, 128), 1)
    req = jnp.full((1, 128), -1, jnp.int32)
    asked = jnp.full((1, 128), blocks, jnp.int32)
    owners = []
    for b in range(blocks):
        persona = jnp.clip(bp[b], 0, ps.shape[0] - 1)
        slot = jnp.clip(ps[persona], 0, ps.shape[0] - 1)
        owner = lax.div(slot, pers)
        pos = sum([(owner == other).astype(jnp.int32) for other in owners], jnp.int32(0))
        pos = jnp.minimum(pos, CAP - 1)
        owners.append(owner)
        here = lane == owner * CAP + pos
        req = jnp.where(here, slot - owner * pers, req)
        asked = jnp.where(here, b, asked)
        owner_y = lax.div(owner, NX)
        rel_y = lax.rem(owner_y - y + ny, ny)
        rel_x = lax.rem(owner - owner_y * NX - x + NX, NX)
        blk_slot[b] = (rel_x * ny + rel_y) * CAP + pos
    rtab_v[0] = req
    asked_v[...] = asked
    ask_to_smem = pltpu.make_async_copy(asked_v, asked_s, local_sem.at[6])
    ask_to_smem.start()

    pl.semaphore_wait(barrier, len(peers))

    steps_p = [ny // 2, ny - 1 - ny // 2]
    steps_m = [ny - 1 - ny // 2, ny // 2]
    ring = {}
    cut = pers // CHUNKS
    parts = [pl.ds(c * cut, cut if c < CHUNKS - 1 else pers - c * cut) for c in range(CHUNKS)]

    def ring_send(h, toward_low, step, c):
        if toward_low:
            src, row, device = tab[h][step - 1], step, at_y(-1)
        else:
            src, row, device = tab[h][(ny - step + 1) % ny], ny - step, at_y(1)
        copy = copies.make(src.at[parts[c]], tab[h][row].at[parts[c]], device)
        copy.start()
        ring[h, toward_low, step, c] = copy

    def ring_steps(h, toward_low):
        return (steps_p if toward_low else steps_m)[h]

    def ring_first(h, toward_low, c):
        if ring_steps(h, toward_low) >= 1:
            ring_send(h, toward_low, 1, c)

    def ring_take(h, step):
        for c in range(CHUNKS):
            for toward_low in (True, False):
                if step > ring_steps(h, toward_low):
                    continue
                ring[h, toward_low, step, c].wait_recv()
                if step < ring_steps(h, toward_low):
                    ring_send(h, toward_low, step + 1, c)
                if h == 0 and step == max(ring_steps(0, toward_low) - 1, 1):
                    ring_first(1, toward_low, c)
        low = [step] if step <= ring_steps(h, True) else []
        return low + ([ny - step] if step <= ring_steps(h, False) else [])

    ask = []
    for d in range(1, NX):
        copy = copies.make(rtab_v.at[0], rtab_v.at[NX - d], at_x(d))
        copy.start()
        ask.append(copy)
    load_up.wait()
    load_down.wait()
    for c in range(CHUNKS):
        ring_first(0, True, c)
        ring_first(0, False, c)
        if steps_m[0] == 0:
            ring_first(1, False, c)
    for copy in ask:
        copy.wait_recv()
    to_smem = pltpu.make_async_copy(rtab_v, rtab_s, local_sem.at[2])
    to_smem.start()
    ctab[0] = rtab_v[...]
    to_smem.wait()
    ask_to_smem.wait()
    table_copies = []
    for d in range(1, ny):
        copy = copies.make(rtab_v, ctab.at[ny - d], at_y(d))
        copy.start()
        table_copies.append(copy)

    def owner_slot(row, rel_x):
        return (lax.rem(y + row, ny) * NX + lax.rem(x + rel_x, NX)) * CAP

    hops = {}

    def land_at(rel_x, row):
        return pl.ds((rel_x * ny + row) * CAP, CAP)

    def x_send(key, land, stage, row):
        for d in (2, 1, 3):
            copy = copies.make(stage[d - 1].at[row], land.at[land_at(NX - d, row)], at_x(d))
            copy.start()
            hops[key, d] = copy

    def x_landed(key):
        for d in range(1, NX):
            hops[key, d].wait_recv()

    def issue_adapters(h, row):
        table = tab[h][row]

        def pick(rel_x, pos):
            return table[jnp.maximum(rtab_s[rel_x, 0, owner_slot(row, 0) + pos], 0)]

        for d in range(1, NX):
            for pos in range(CAP):
                sx[h][d - 1][row, pos] = pick(d, pos)
        x_send(("a", h, row), rx[h], sx[h], row)
        for pos in range(CAP):
            rx[h][row * CAP + pos] = pick(0, pos)

    def issue_gradients(h, row):
        for d in range(1, NX):
            for pos in range(CAP):
                bs[h][d - 1][row, pos] = grads[h][asked_s[0, owner_slot(row, d) + pos]]
        x_send(("g", h, row), gr[h], bs[h], row)

    sums = {}

    def row_sum(h, row, k):
        base = owner_slot(row, 0)
        total = jnp.zeros((rank, gup.shape[2]), F32)
        terms = []
        for rel_x in range(1, NX):
            for pos in range(CAP):
                place = (rel_x * ny + row) * CAP + pos
                terms.append((rtab_s[rel_x, 0, base + pos], gr[h][place]))
        for pos in range(CAP):
            terms.append((rtab_s[0, 0, base + pos], grads[h][asked_s[0, base + pos]]))
        for asked, term in terms:
            total += jnp.where(asked == k, term.astype(F32), 0.0)
        return total

    back_p = [steps_p[1], steps_p[0]]
    back_m = [steps_m[1], steps_m[0]]

    def back_place(h, row):
        j = ny - row
        return (True, j) if j <= back_p[h] else (False, row)

    def back_slot(toward_low, j):
        return j - 1 if toward_low else ny - 1 - j

    def back_order(h):
        order = []
        for j in range(ny // 2, 0, -1):
            order += [ny - j] if j <= back_p[h] else []
            order += [j] if j <= back_m[h] else []
        return order + [0]

    def finish_gradients(h, row):
        x_landed(("g", h, row))
        if row == 0:
            return
        toward_low, j = back_place(h, row)
        last = j == (back_p if toward_low else back_m)[h]
        farther = None if last else yr[h][back_slot(toward_low, j + 1)]
        out = ys[h][back_slot(toward_low, j)]
        land = yr[h][back_slot(toward_low, j)]

        def one(k, _):
            total = row_sum(h, row, k)
            if farther is not None:
                total += farther[k].astype(F32)
            out[k] = total.astype(BF16)
            return 0

        for c, part in enumerate(parts):
            if not last:
                sums[h, toward_low, j + 1, c].wait_recv()
            lax.fori_loop(part.start, part.start + part.size, one, 0)
            copy = copies.make(out.at[part], land.at[part], at_y(-1 if toward_low else 1))
            copy.start()
            sums[h, toward_low, j, c] = copy

    def write_gradients(h):
        nearest = []
        for toward_low in (True, False):
            if (back_p if toward_low else back_m)[h] >= 1:
                for c in range(CHUNKS):
                    sums[h, toward_low, 1, c].wait_recv()
                nearest.append(yr[h][back_slot(toward_low, 1)])
        mine = lane // CAP == dp
        for k in range(pers):
            hits = jnp.zeros((1, 128), F32)
            for other in range(ny):
                for rel_x in range(NX):
                    hits += jnp.where(mine & (ctab[other, rel_x] == k), 1.0, 0.0)
            count = jnp.sum(hits, axis=1, keepdims=True)
            scaling = ADAPTER_SCALE / (act.shape[1] * jnp.maximum(count, 1.0))
            total = row_sum(h, 0, k)
            for ref in nearest:
                total += ref[k].astype(F32)
            total = total * scaling
            if h == 0:
                gdn[k] = total.astype(BF16)
            else:
                gup[k] = total.astype(BF16)

    half = pad_blocks * rank // 2
    chunk = half // nz
    tensor_copies = {}

    def rows_of(c, zz):
        return pl.ds(pl.multiple_of(c * half + zz * chunk, 16), chunk)

    def project(h):
        if h == 0:
            load_cot.wait()
        for row in range(ny):
            x_landed(("a", h, row))
        tokens = cot_v if h == 0 else act_v

        def one(b, _):
            weights = rx[h][blk_slot[b]]
            part[h][pl.ds(pl.multiple_of(b * rank, rank), rank), :] = lax.dot_general(
                weights, tokens[b], (((1,), (1,)), ((), ())), preferred_element_type=F32
            )
            return 0

        lax.fori_loop(0, blocks, one, 0, unroll=2)
        if pad_blocks > blocks:
            part[h][pl.ds(blocks * rank, (pad_blocks - blocks) * rank), :] = jnp.zeros(
                ((pad_blocks - blocks) * rank, part[h].shape[1]), F32
            )
        copy = copies.make(
            part[h].at[pl.ds(pl.multiple_of((1 - core) * half, 16), half)], pair[h], sibling
        )
        copy.start()
        tensor_copies[h, "pair"] = copy

    def scatter(h):
        tensor_copies[h, "pair"].wait_recv()

        def one(zz, _):
            rows = pl.ds(pl.multiple_of(zz * chunk, 16), chunk)
            zs[h][rows, :] = (part[h][rows_of(core, zz), :] + pair[h][rows, :]).astype(BF16)
            return 0

        lax.fori_loop(0, nz, one, 0)
        for d in range(1, nz):
            other = lax.rem(z + d, nz)
            copy = copies.make(
                zs[h].at[pl.ds(pl.multiple_of(other * chunk, 16), chunk)], zr[h].at[d - 1], at_z(d)
            )
            copy.start()
            tensor_copies[h, "scatter", d] = copy

    def gather(h):
        own = pl.ds(pl.multiple_of(z * chunk, 16), chunk)
        total = part[h][rows_of(core, z), :] + pair[h][own, :]
        for d in range(1, nz):
            tensor_copies[h, "scatter", d].wait_recv()
            total += zr[h][d - 1].astype(F32)
        mine = rows_of(core, z)
        full[h][mine, :] = total.astype(BF16)
        for d in range(1, nz):
            copy = copies.make(full[h].at[mine], full[h].at[mine], at_z(d))
            copy.start()
            tensor_copies[h, "gather", d] = copy
        share_chunk(h, 0)

    def share_chunk(h, d):
        rows = rows_of(core, lax.rem(z - d + nz, nz))
        copy = copies.make(full[h].at[rows], full[h].at[rows], sibling)
        copy.start()
        tensor_copies[h, "share", d] = copy

    def share(h):
        for d in range(1, nz):
            tensor_copies[h, "gather", d].wait_recv()
            share_chunk(h, d)

    def ranks(h, b):
        return full[h][pl.ds(pl.multiple_of(b * rank, rank), rank), :]

    def block_gradients(h):
        for d in range(nz):
            tensor_copies[h, "share", d].wait_recv()
        if h == 0:
            load_act.wait()
        tokens = act_v if h == 0 else cot_v
        grads[h][blocks] = jnp.zeros(grads[h].shape[1:], BF16)

        def one(b, _):
            grads[h][b] = jnp.dot(ranks(h, b), tokens[b], preferred_element_type=F32).astype(BF16)
            return 0

        lax.fori_loop(0, blocks, one, 0, unroll=2)

    store_gi = pltpu.make_async_copy(gi_v, gi, local_sem.at[3])

    def input_gradient():
        def one(b, _):
            weights = rx[1][blk_slot[b]]
            gi_v[b] = (
                ADAPTER_SCALE
                * lax.dot_general(
                    ranks(0, b), weights, (((0,), (0,)), ((), ())), preferred_element_type=F32
                )
            ).astype(BF16)
            return 0

        lax.fori_loop(0, blocks, one, 0, unroll=2)
        store_gi.start()

    issue_adapters(0, 0)
    for s in range(1, ny // 2 + 1):
        for row in ring_take(0, s):
            issue_adapters(0, row)
    issue_adapters(1, 0)
    for copy in table_copies:
        copy.wait_recv()
    beside = [(2, project), (3, scatter), (4, gather), (4, share), (99, block_gradients)]
    for s in range(1, ny // 2 + 1):
        for row in ring_take(1, s):
            issue_adapters(1, row)
        while s >= beside[0][0]:
            beside.pop(0)[1](0)
    for _, what in beside:
        what(0)
    early = len(copies.all)
    orders = [back_order(0), back_order(1)]
    for row in orders[0][: ny // 2]:
        issue_gradients(0, row)
    project(1)
    for row in orders[0][ny // 2 :]:
        issue_gradients(0, row)
    scatter(1)

    def turn():
        block_gradients(1)
        for row in orders[1]:
            issue_gradients(1, row)
        copies.flush(early)

    beside = [
        (1, lambda: gather(1)), (2, input_gradient), (3, lambda: share(1)), (4, turn),
    ]
    for i, row in enumerate(orders[0]):
        finish_gradients(0, row)
        while beside and i >= beside[0][0]:
            beside.pop(0)[1]()
    for _, what in beside:
        what()
    write_gradients(0)
    middle = len(copies.all)
    for i, row in enumerate(orders[1]):
        if i == ny - 2:
            copies.flush(middle)
        finish_gradients(1, row)
    write_gradients(1)
    copies.flush(len(copies.all))
    store_gi.wait()
    assert copies.used == copy_count(ny, nz)


def step(ny, nz, activations, cotangent, down_adapters, up_adapters, block_persona, persona_slot):
    blocks = block_persona.shape[0]
    block = activations.shape[0] // blocks
    features = activations.shape[1]
    pers, rank = up_adapters.shape[:2]
    smem = pl.BlockSpec(memory_space=pltpu.SMEM)
    vmem = pl.BlockSpec(memory_space=pltpu.VMEM)
    anywhere = pl.BlockSpec(memory_space=pl.ANY)
    unit = CORES * nz * 16
    pad_blocks = blocks
    while pad_blocks * rank % unit:
        pad_blocks += 1
    rows = pad_blocks * rank
    adapter = (rank, features)

    def bf16(*shape):
        return pltpu.VMEM(shape, BF16)

    def f32(*shape):
        return pltpu.VMEM(shape, F32)

    scratch = [bf16(blocks, block, features)] * 3
    landing = NX * ny * CAP
    scratch += [bf16(pers, *adapter)] * (2 * ny)
    scratch += [bf16(landing, *adapter)] * 2
    scratch += [bf16(ny, CAP, *adapter)] * (2 * (NX - 1))
    scratch += [bf16(blocks + 1, *adapter)] * 2
    scratch += [bf16(landing, *adapter)] * 2
    scratch += [bf16(ny, CAP, *adapter)] * (2 * (NX - 1))
    scratch += [bf16(pers, *adapter)] * (4 * (ny - 1))
    scratch += [f32(rows, block)] * 2 + [f32(rows // 2, block)] * 2
    scratch += [bf16(rows // 2, block)] * 2
    scratch += [bf16(max(nz - 1, 1), rows // 2 // nz, block)] * 2
    scratch += [bf16(rows, block)] * 2
    scratch += [
        pltpu.VMEM((NX, 1, 128), jnp.int32),
        pltpu.SMEM((NX, 1, 128), jnp.int32),
        pltpu.VMEM((ny, NX, 1, 128), jnp.int32),
        pltpu.VMEM((1, 128), jnp.int32),
        pltpu.SMEM((1, 128), jnp.int32),
        pltpu.SMEM((blocks,), jnp.int32),
    ]
    n = copy_count(ny, nz)
    scratch += [pltpu.SemaphoreType.DMA((n,)), pltpu.SemaphoreType.DMA((n,)), pltpu.SemaphoreType.DMA((7,))]
    gi, gdn, gup = pl.pallas_call(
        functools.partial(main_kernel, (ny, nz, pers, blocks, pad_blocks, rank)),
        out_shape=(
            jax.ShapeDtypeStruct((blocks, block, features), BF16),
            jax.ShapeDtypeStruct(up_adapters.shape, BF16),
            jax.ShapeDtypeStruct(up_adapters.shape, BF16),
        ),
        in_specs=[smem, smem] + [anywhere] * 4,
        out_specs=(anywhere, vmem, vmem),
        scratch_shapes=scratch,
        compiler_params=pltpu.CompilerParams(
            collective_id=0, has_side_effects=True, vmem_limit_bytes=56 * 2**20
        ),
    )(
        block_persona, persona_slot, up_adapters, jnp.swapaxes(down_adapters, 1, 2),
        activations.reshape(blocks, block, features), cotangent.reshape(blocks, block, features),
    )
    return gi.reshape(activations.shape), jnp.swapaxes(gdn, 1, 2), gup


def solution(mesh):
    ny, nz = mesh.shape["dp"] // NX, mesh.shape["tensor"] // CORES
    return jax.shard_map(
        functools.partial(step, ny, nz),
        mesh=mesh,
        in_specs=(
            P("dp", "tensor"),
            P("dp", "tensor"),
            P("dp", "tensor", None),
            P("dp", None, "tensor"),
            P("dp"),
            P(),
        ),
        out_specs=(P("dp", "tensor"), P("dp", "tensor", None), P("dp", None, "tensor")),
        check_vma=False,
    )
```
